128 devices in a mesh: role: 8 (over z, core), dev: 16 (over y, x).
Axes of the slice: x: 4, y: 4, z: 4, core: 2. Of those that a mesh axis runs over, the one named last changes fastest.
Arguments:
- hidden_rows: bfloat16 [16384, 21504], P(('role', 'dev')), may hold values from -6 to 6
- lengths: int32 [128, 4], P(('role', 'dev')), may hold values from 1 to 32, as said below
- balance: int32 [4096, 1], P(('role', 'dev')), may hold values from 0 to 7; in each aligned block of 32 rows (0 to 31, 32 to 63, ...) at most 5 rows name the same one
- cotangent: bfloat16 [20480, 3584], P(('role', 'dev')), may hold values from -0.046875 to 0.046875
Outputs:
- grad_weight: float32 [3584, 21504], P('role', 'dev')
The draws below stay inside these ranges and needn't reach their ends.
Inputs may be any that keep to these rules, and one draw needn't show every extreme that they name: `lengths`: on every device one slot has length exactly 32. `balance`: the 32 blocks of one device send at most 5 blocks to one draft group; in every draw some device sends exactly 5 blocks to one group.
All inputs are finite; a program needn't handle non-finite values.
Results may differ from the reference program's by a relative error of at most 0.0003.
Values may be sent and summed in bfloat16 or wider, within the bound.
No kernel may reach another device: no remote copies, remote signals or barrier semaphores. Data moves between devices by JAX's collectives and lax.ppermute only.
A program may use at most 192 MiB of HBM per device.

```python
import math
import jax
import jax.numpy as jnp
import numpy as np
from jax import lax

K = 21504
C = 3584
TOK_DEV = 128
SEQ_DEV = 4
BLK = 4
SLOT = 32
NB = 32
CAP = 5
SLOTS = 160
N_ROLE = 8
N_DEV = 16


def draw_lengths(key, part):
    key = jax.random.fold_in(key, 11)
    first_key, second_key, third_key = jax.random.split(key, 3)
    shape = (N_ROLE * N_DEV, SEQ_DEV)
    first_len = jax.random.randint(first_key, shape, 1, SLOT + 1)
    second_len = jax.random.randint(second_key, shape, 1, SLOT + 1)
    shorter = jnp.minimum(first_len, second_len)
    picked = jax.random.randint(third_key, (N_ROLE * N_DEV,), 0, SEQ_DEV)
    filled = jax.lax.broadcasted_iota(jnp.int32, shape, 1) == picked[:, None]
    return jnp.where(filled, SLOT, shorter).astype(jnp.int32)


def shard_levels(own_key, dims, shards, least, largest):
    factor_of = 1.0
    for axis_at, blocks in shards:
        draws = jax.random.uniform(jax.random.fold_in(jax.random.fold_in(own_key, 6), axis_at), (blocks,), jnp.float32, least / len(shards), largest / len(shards))
        factor_of = factor_of * jnp.repeat(jnp.exp(draws), dims[axis_at] // blocks).reshape((-1,) + (1,) * (len(dims) - 1 - axis_at))
    return factor_of


def deal_out(stream_key, own, number, rows, count, top, limit, slope):
    sequence = jax.random.permutation(stream_key, count)
    packed, common = shares(count, rows * top, limit, slope, True), shares(count, rows * top, limit, slope, False)
    places = jnp.arange(count)

    def named(tallies, turn):
        used = int((tallies > 0).sum())
        fixed = max(1, used // 4)
        passed = fixed + (places - fixed + turn * (used - fixed)) % max(1, count - fixed)
        return jnp.zeros((count,), jnp.int32).at[sequence[jnp.where(places < fixed, places, passed)]].set(jnp.asarray(tallies, jnp.int32))

    tallies = jnp.where(number % 4 == 0, named(packed, number // 4), named(common, number - number // 4 - 1))
    mixed = jax.random.permutation(jax.random.fold_in(own, 3), count)
    donor, receiver = mixed[0:count // 2 * 2:2], mixed[1:count // 2 * 2:2]
    margin = jnp.minimum(tallies[donor] - 1, limit - tallies[receiver]) // 2
    margin = jnp.where((donor == sequence[0]) | (receiver == sequence[0]) | (tallies[receiver] == 0), 0, jnp.maximum(margin, 0))
    passed = jax.random.randint(jax.random.fold_in(own, 4), (count // 2,), 0, 1 << 20) % (margin + 1)
    tallies = tallies.at[donor].add(-passed).at[receiver].add(passed)
    items = jnp.searchsorted(jnp.cumsum(tallies), jnp.arange(rows * top), side="right").astype(jnp.int32)
    listing = items.reshape(top, rows).T
    listing = listing[jax.random.permutation(jax.random.fold_in(own, 1), rows)]
    turn = jax.random.randint(jax.random.fold_in(own, 2), (rows, 1), 0, top)
    return jnp.take_along_axis(listing, (jnp.arange(top)[None, :] + turn) % top, axis=1)


def shares(number_of, total, reach, slope, full):
    loads = [(1 << 20) // math.isqrt(rank ** slope) + 1 for rank in range(1, number_of + 1)]
    largest = reach if full else min(reach, max(-(-total // number_of), total * loads[0] // sum(loads)))
    least = 1 if total - largest >= number_of - 1 else 0
    given, spare = [largest] + [least] * (number_of - 1), total - largest - least * (number_of - 1)
    while spare > 0:
        movable = [i for i in range(1, number_of) if given[i] < largest] or [i for i in range(1, number_of) if given[i] < reach]
        pool, budget = sum([loads[i] for i in movable]), spare
        for i in movable:
            extra = min(reach - given[i], max(1, budget * loads[i] // pool), spare)
            given[i] = given[i] + extra
            spare = spare - extra
    return np.array(given)


def noise(key, shape, width, bound, pieces=(), kind=jnp.bfloat16):
    loudness = shard_levels(key, shape, pieces, -0.22, 0.18) if pieces else 1.0
    entries = jax.random.normal(key, shape, jnp.float32) * width * loudness
    return jnp.minimum(jnp.maximum(entries, -bound), bound).astype(kind)


def setup_inputs(seed: int = 0) -> dict:
    seeds = jax.random.split(jax.random.key(seed), 5)
    hidden_rows = noise(seeds[0], (N_ROLE * N_DEV * TOK_DEV, K), 1.0, 6.0, ((0, 128),))
    lengths = draw_lengths(jax.random.fold_in(seeds[4], 71), 0)
    balance_keys = jax.random.split(jax.random.fold_in(seeds[2], 1), (N_ROLE * N_DEV * NB) // NB)
    balance_turns = jax.random.permutation(jax.random.fold_in(seeds[2], 3), (N_ROLE * N_DEV * NB) // NB)
    balance = jax.vmap(lambda own, number: deal_out(jax.random.fold_in(seeds[2], 2), own, number, NB, N_ROLE, 1, CAP, 2))(balance_keys, balance_turns).reshape((N_ROLE * N_DEV * NB, 1))
    cotangent = noise(seeds[3], (N_ROLE * N_DEV * SLOTS, C), (N_ROLE * N_DEV * TOK_DEV) ** -0.5, 0.046875, ((0, 128),))
    return {"hidden_rows": hidden_rows, "lengths": lengths, "balance": balance, "cotangent": cotangent}


def reference(hidden_rows, lengths, balance, cotangent):
    source_count = N_ROLE * N_DEV
    positions = jnp.arange(TOK_DEV, dtype=jnp.int32) % SLOT
    slot_of_row = jnp.arange(TOK_DEV, dtype=jnp.int32) // SLOT
    row_lengths = lengths[:, slot_of_row]
    keeping = positions[None, :] < row_lengths
    stacked = hidden_rows.reshape(source_count, TOK_DEV, K)
    masked = jnp.where(keeping[:, :, None], stacked, jnp.zeros_like(stacked))
    blocks = masked.reshape(source_count, NB, BLK, K)
    groups = balance.reshape(source_count, NB)
    onehot = (groups[:, :, None] == jnp.arange(N_ROLE, dtype=jnp.int32)[None, None, :]).astype(jnp.int32)
    earlier = jnp.cumsum(onehot, axis=1) - onehot
    block_rank = jnp.sum(earlier * onehot, axis=2)
    block_ids = jnp.arange(NB, dtype=jnp.int32)
    cap_ids = jnp.arange(CAP, dtype=jnp.int32)
    paired_cot = cotangent.reshape(N_ROLE, N_DEV, N_ROLE, CAP * BLK, C)

    def add_group(group, running):
        group_id = jnp.asarray(group).astype(jnp.int32)
        chosen = (groups[:, :, None] == group_id) & (block_rank[:, :, None] == cap_ids[None, None, :])
        present = jnp.any(chosen, axis=1)
        picked = jnp.sum(jnp.where(chosen, block_ids[None, :, None], jnp.zeros_like(block_ids)[None, :, None]), axis=1).astype(jnp.int32)
        taken = jnp.take_along_axis(blocks, picked[:, :, None, None], axis=1)
        taken = jnp.where(present[:, :, None, None], taken, jnp.zeros_like(taken))
        slot_rows = taken.reshape(N_ROLE, N_DEV, CAP * BLK, K).transpose(1, 0, 2, 3).reshape(-1, K)
        group_cot = lax.dynamic_index_in_dim(paired_cot, group_id, 0, keepdims=False).reshape(-1, C)
        partial_value = jnp.dot(group_cot.T, slot_rows, preferred_element_type=jnp.float32)
        return running + partial_value

    return lax.fori_loop(0, N_ROLE, add_group, jnp.zeros((C, K), jnp.float32))
```

```python
import functools

import jax
import jax.numpy as jnp
from jax import lax
from jax.experimental import pallas as pl
from jax.experimental.pallas import tpu as pltpu
from jax.sharding import PartitionSpec as P

PARTS = 4
FIRST_COLS = 384


def windows(hidden_rows, starts, width):
    tok_count = hidden_rows.shape[0]
    dev_count = len(starts)
    step = starts[2] - starts[0]
    first, second = starts[0], starts[1] - starts[0]

    def kernel(rows_ref, out_ref):
        out_ref[0] = rows_ref[...]

    def where(i):
        return 0, pl.multiple_of(first + (i // 2) * step + (i % 2) * second, 128)

    return pl.pallas_call(
        kernel,
        grid=(dev_count,),
        in_specs=[pl.BlockSpec((pl.Element(tok_count), pl.Element(width)), where)],
        out_specs=pl.BlockSpec((1, tok_count, width), lambda i: (i, 0, 0)),
        out_shape=jax.ShapeDtypeStruct((dev_count, tok_count, width), hidden_rows.dtype),
        name="cut_windows",
    )(hidden_rows)


def sort_blocks(cotangent, targets, role_count):
    rows, width = cotangent.shape
    block = rows // role_count
    cols = width // 4

    def kernel(targets_ref, cot_ref, *out_refs):
        for j in range(role_count):
            row = lax.broadcasted_iota(jnp.int32, (block, rows), 0)
            column = lax.broadcasted_iota(jnp.int32, (block, rows), 1)
            taking = (column == row + targets_ref[j] * block).astype(jnp.bfloat16)
            out_refs[j][...] = jnp.dot(
                taking, cot_ref[...], preferred_element_type=jnp.float32
            ).astype(jnp.bfloat16)

    return pl.pallas_call(
        kernel,
        grid=(4,),
        in_specs=[
            pl.BlockSpec(memory_space=pltpu.SMEM),
            pl.BlockSpec((rows, cols), lambda i: (0, i)),
        ],
        out_specs=[pl.BlockSpec((block, cols), lambda i: (0, i))] * role_count,
        out_shape=[jax.ShapeDtypeStruct((block, width), cotangent.dtype)] * role_count,
        name="sort_blocks",
    )(targets, cotangent)


def pair_rows(blocks, places, role_count, parts):
    block, width = blocks[0].shape
    count = len(blocks)
    tok_count = places.shape[2]
    share = width // role_count
    piece = share // parts
    fold = 2

    def kernel(places_ref, *refs):
        ins, outs = refs[:count], refs[count:]
        total = jnp.zeros((fold * share, tok_count), jnp.float32)
        for j in range(count):
            total += lax.dot_general(
                ins[j][...],
                places_ref[j],
                (((0,), (0,)), ((), ())),
                preferred_element_type=jnp.float32,
            )
        total = total.astype(jnp.bfloat16)
        for p in range(parts):
            for q in range(fold):
                at = q * share + p * piece
                outs[p][q * piece : (q + 1) * piece] = total[at : at + piece]

    return pl.pallas_call(
        kernel,
        grid=(role_count // fold,),
        in_specs=[pl.BlockSpec((count, block, tok_count), lambda i: (0, 0, 0))]
        + [pl.BlockSpec((block, fold * share), lambda i: (0, i))] * count,
        out_specs=[pl.BlockSpec((fold * piece, tok_count), lambda i: (i, 0))] * parts,
        out_shape=[jax.ShapeDtypeStruct((role_count * piece, tok_count), jnp.bfloat16)] * parts,
        name="pair_rows",
    )(places, *blocks)


def multiply(cot, features, tile):
    source_count, depth, tok_count = cot.shape
    width = sum(f.shape[2] for f in features)

    def kernel(cot_ref, *refs):
        left = jnp.concatenate([cot_ref[s] for s in range(source_count)], axis=1)
        at = 0
        for f_ref in refs[:-1]:
            f = f_ref[...].reshape(source_count * tok_count, f_ref.shape[2])
            refs[-1][:, at : at + f.shape[1]] = jnp.dot(left, f, preferred_element_type=jnp.float32)
            at += f.shape[1]

    return pl.pallas_call(
        kernel,
        grid=(depth // tile,),
        in_specs=[pl.BlockSpec((source_count, tile, tok_count), lambda i: (0, i, 0))]
        + [pl.BlockSpec(f.shape, lambda i: (0, 0, 0)) for f in features],
        out_specs=pl.BlockSpec((tile, width), lambda i: (i, 0)),
        out_shape=jax.ShapeDtypeStruct((depth, width), jnp.float32),
        compiler_params=pltpu.CompilerParams(vmem_limit_bytes=48 * 1024 * 1024),
        cost_estimate=pl.CostEstimate(
            flops=2 * depth * width * source_count * tok_count,
            bytes_accessed=depth * width * 4 + source_count * tok_count * (width + depth) * 2,
            transcendentals=0,
        ),
        name="multiply",
    )(cot, *features)


def finish(pieces, shift, odd, width):
    rows = pieces[0].shape[0]
    count = len(pieces)

    def kernel(odd_ref, *refs):
        for p in range(count):
            even_cols = refs[p][:, :width]
            odd_cols = refs[p][:, shift : shift + width]
            refs[-1][p * rows : (p + 1) * rows] = jnp.where(odd_ref[0] == 1, odd_cols, even_cols)

    return pl.pallas_call(
        kernel,
        in_specs=[pl.BlockSpec(memory_space=pltpu.SMEM)]
        + [pl.BlockSpec(memory_space=pltpu.VMEM)] * count,
        out_specs=pl.BlockSpec(memory_space=pltpu.VMEM),
        out_shape=jax.ShapeDtypeStruct((rows * count, width), jnp.float32),
        compiler_params=pltpu.CompilerParams(vmem_limit_bytes=32 * 1024 * 1024),
        name="finish",
    )(odd, *pieces)


def body(hidden_rows, lengths, balance, cotangent):
    role_count = lax.axis_size("role")
    dev_count = lax.axis_size("dev")
    role, dev = lax.axis_index("role"), lax.axis_index("dev")
    tok_count, width_in = hidden_rows.shape
    seq_count = lengths.shape[1]
    slot_len = tok_count // seq_count
    block_count = balance.shape[0]
    block_rows = tok_count // block_count
    pair_count = cotangent.shape[0] // role_count
    capacity = pair_count // block_rows
    slice_width = width_in // dev_count
    shift = slice_width % 128
    window = slice_width + shift
    starts = [slice_width * d - shift * (d % 2) for d in range(dev_count)]

    hops = jnp.arange(role_count, dtype=jnp.int32)
    blocks = sort_blocks(cotangent, (role + hops) % role_count, role_count)
    blocks = [blocks[0]] + [
        lax.ppermute(
            blocks[j], "role", [(r, (r + j) % role_count) for r in range(role_count)]
        )
        for j in range(1, role_count)
    ]

    groups = balance[:, 0]
    onehot = (groups[:, None] == hops[None, :]).astype(jnp.int32)
    earlier = jnp.cumsum(onehot, axis=0) - onehot
    block_rank = jnp.sum(earlier * onehot, axis=1)
    token = jnp.arange(tok_count, dtype=jnp.int32)
    row_of_token = jnp.repeat(block_rank, block_rows) * block_rows + token % block_rows
    group_of_token = jnp.repeat(groups, block_rows)
    keeping = token % slot_len < jnp.repeat(lengths[0], slot_len)
    rows = jnp.arange(pair_count, dtype=jnp.int32)
    from_group = (role - hops) % role_count
    places = (
        (from_group[:, None, None] == group_of_token[None, None, :])
        & (rows[None, :, None] == row_of_token[None, None, :])
        & keeping[None, None, :]
    ).astype(jnp.bfloat16)

    early = windows(hidden_rows, starts, FIRST_COLS)
    late = windows(hidden_rows, [s + FIRST_COLS for s in starts], window - FIRST_COLS)
    exchange = functools.partial(
        lax.all_to_all, axis_name="dev", split_axis=0, concat_axis=0, tiled=True
    )
    early = exchange(early)
    blocks = lax.optimization_barrier((blocks, early))[0]
    paired = pair_rows(blocks, places, role_count, PARTS)
    paired, late = lax.optimization_barrier((paired, late))
    gathered = [lax.all_gather(p, "dev", axis=0, tiled=False) for p in paired]
    late = exchange(late)

    pieces = []
    for cot in gathered:
        partial = multiply(cot, [early, late], cot.shape[1] // 4)
        pieces.append(lax.psum_scatter(partial, "role", scatter_dimension=0, tiled=True))
    return finish(pieces, shift, (dev % 2).reshape(1), slice_width)


def solution(mesh):
    in_specs = (
        P(("role", "dev"), None),
        P(("role", "dev"), None),
        P(("role", "dev"), None),
        P(("role", "dev"), None),
    )
    out_specs = P("role", "dev")
    return jax.shard_map(body, mesh=mesh, in_specs=in_specs, out_specs=out_specs, check_vma=False)
```

```python
import jax
import jax.numpy as jnp
from jax import lax
from jax.experimental import pallas as pl
from jax.experimental.pallas import tpu as pltpu
from jax.sharding import PartitionSpec as P

PARTS = (224, 224)
STEP = 112
SPANS = (512, 896)
FINE = 256.0
TOP = 32767.0
SIDE = 4
VMEM = pl.BlockSpec(memory_space=pltpu.VMEM)
SMEM = pl.BlockSpec(memory_space=pltpu.SMEM)
ANY = pl.BlockSpec(memory_space=pl.ANY)
TINY = pl.CostEstimate(flops=1, bytes_accessed=1, transcendentals=0)


def params(mib):
    return pltpu.CompilerParams(vmem_limit_bytes=mib * 1024 * 1024)


def along_z(step, flip=0):
    return [
        (z * 2 + c, (z + step) % SIDE * 2 + (c + flip) % 2) for z in range(SIDE) for c in range(2)
    ]


def cut_windows(hidden_rows, starts, width):
    tok_count, width_in = hidden_rows.shape
    tile = 32

    def kernel(rows_ref, out_ref):
        for d, start in enumerate(starts):
            out_ref[d] = rows_ref[:, start : start + width]

    return pl.pallas_call(
        kernel,
        grid=(tok_count // tile,),
        in_specs=[pl.BlockSpec((tile, width_in), lambda i: (i, 0))],
        out_specs=pl.BlockSpec((len(starts), tile, width), lambda i: (0, i, 0)),
        out_shape=jax.ShapeDtypeStruct((len(starts), tok_count, width), hidden_rows.dtype),
        compiler_params=params(60),
        name="cut_windows",
    )(hidden_rows)


def hold(value, awaited):
    def kernel(value_ref, awaited_ref, out_ref):
        pass

    return pl.pallas_call(
        kernel,
        in_specs=[ANY, ANY],
        out_specs=ANY,
        out_shape=jax.ShapeDtypeStruct(value.shape, value.dtype),
        input_output_aliases={0: 0},
        compiler_params=params(60),
        cost_estimate=TINY,
        name="hold",
    )(value, awaited)


def sort_blocks(cotangent, targets):
    rows, width = cotangent.shape
    count = targets.shape[0]
    block = rows // count

    def kernel(targets_ref, cot_ref, *out_refs):
        row = lax.broadcasted_iota(jnp.int32, (block, rows), 0)
        column = lax.broadcasted_iota(jnp.int32, (block, rows), 1)
        for j in range(count):
            taking = (column == row + targets_ref[j] * block).astype(jnp.bfloat16)
            out_refs[j][...] = jnp.dot(
                taking, cot_ref[...], preferred_element_type=jnp.float32
            ).astype(jnp.bfloat16)

    return pl.pallas_call(
        kernel,
        in_specs=[SMEM, VMEM],
        out_specs=[VMEM] * count,
        out_shape=[jax.ShapeDtypeStruct((block, width), cotangent.dtype)] * count,
        compiler_params=params(60),
        name="sort_blocks",
    )(targets, cotangent)


def pair_rows(core, blocks, places, *awaited):
    block, width = blocks[0].shape
    count = len(blocks)
    tok_count = places.shape[2]
    share = width // count

    def kernel(core_ref, places_ref, *refs):
        ins, outs = refs[:count], refs[-len(PARTS) :]
        z = pl.program_id(0)
        total = jnp.zeros((2 * share, tok_count), jnp.float32)
        for j in range(count):
            total += lax.dot_general(
                ins[j][...],
                places_ref[j],
                (((0,), (0,)), ((), ())),
                preferred_element_type=jnp.float32,
            )
        total = total.astype(jnp.bfloat16)
        for q in range(2):
            own = jnp.where(core_ref[0] == q, 1, 0)
            at = q * share
            for m, out in zip(PARTS, outs, strict=True):
                to = pl.multiple_of((own * SIDE + z) * m, 16)
                out[pl.ds(to, m)] = total[at : at + m]
                at += m

    return pl.pallas_call(
        kernel,
        grid=(SIDE,),
        in_specs=[SMEM, pl.BlockSpec((count, block, tok_count), lambda i: (0, 0, 0))]
        + [pl.BlockSpec((block, 2 * share), lambda i: (0, i))] * count
        + [ANY] * len(awaited),
        out_specs=[pl.BlockSpec((count * m, tok_count), lambda i: (0, 0)) for m in PARTS],
        out_shape=[jax.ShapeDtypeStruct((count * m, tok_count), jnp.bfloat16) for m in PARTS],
        compiler_params=params(60),
        name="pair_rows",
    )(core, places, *blocks, *awaited)


def multiply(cot, features, *awaited):
    source_count, rows, tok_count = cot.shape
    width = sum(f.shape[2] for f in features)
    steps = 4
    tile = rows // steps

    def kernel(cot_ref, *refs):
        left = jnp.concatenate([cot_ref[i] for i in range(source_count)], axis=1)

        def dots(out):
            at = 0
            for f_ref in refs[: len(features)]:
                span = f_ref.shape[2]
                right = f_ref[...].reshape(source_count * tok_count, span)
                out[:, at : at + span] = jnp.dot(left, right, preferred_element_type=jnp.float32)
                at += span

        for core, out in enumerate(refs[-2:]):

            @pl.when(pl.program_id(0) // (steps // 2) == core)
            def _(out=out):
                dots(out)

    return pl.pallas_call(
        kernel,
        grid=(steps,),
        in_specs=[pl.BlockSpec((source_count, tile, tok_count), lambda i: (0, i, 0))]
        + [pl.BlockSpec(f.shape, lambda i: (0, 0, 0)) for f in features]
        + [ANY] * len(awaited),
        out_specs=[
            pl.BlockSpec((tile, width), lambda i: (jnp.minimum(i, steps // 2 - 1), 0)),
            pl.BlockSpec((tile, width), lambda i: (jnp.maximum(i - steps // 2, 0), 0)),
        ],
        out_shape=[jax.ShapeDtypeStruct((steps // 2 * tile, width), jnp.float32)] * 2,
        compiler_params=params(60),
        cost_estimate=TINY,
        name="multiply",
    )(cot, *features, *awaited)


def code(own, got, *awaited):
    rows, width = own.shape
    m = rows // SIDE

    def kernel(own_ref, got_ref, *refs):
        out = refs[-1]
        total = own_ref[...] + got_ref[...]
        largest = jnp.max(jnp.abs(total), axis=0, keepdims=True)
        level = jnp.ceil(jnp.log2(jnp.maximum(largest, 2.0**-125)) * FINE) + 1.0
        scaled = (total * jnp.exp2(level * (-1.0 / FINE))) * TOP
        coded = jnp.round(jnp.clip(scaled, -TOP, TOP)).astype(jnp.int32)
        out[0, :m] = coded.astype(jnp.int16)
        out[0, m:] = jnp.broadcast_to(level.astype(jnp.int32), (16, width)).astype(jnp.int16)

    return pl.pallas_call(
        kernel,
        grid=(SIDE,),
        in_specs=[pl.BlockSpec((m, width), lambda i: (i, 0))] * 2 + [ANY] * len(awaited),
        out_specs=pl.BlockSpec((1, m + 16, width), lambda i: (i, 0, 0)),
        out_shape=jax.ShapeDtypeStruct((SIDE, m + 16, width), jnp.int16),
        compiler_params=params(60),
        cost_estimate=TINY,
        name="code",
    )(own, got, *awaited)


def finish(parts, odd, shift, width):
    counts = [m // STEP for m in PARTS]
    firsts = [sum(counts[:p]) for p in range(len(counts))]

    def kernel(odd_ref, *refs):
        out = refs[-1]
        for p, (first, count) in enumerate(zip(firsts, counts, strict=True)):
            rows, levels = refs[2 * p], refs[2 * p + 1]

            @pl.when((pl.program_id(0) >= first) & (pl.program_id(0) < first + count))
            def _(rows=rows, levels=levels):
                total = 0.0
                for z in range(SIDE):
                    level = levels[z].astype(jnp.int32).astype(jnp.float32)[:1]
                    scale = jnp.exp2(level * (1.0 / FINE)) * (1.0 / TOP)
                    total = total + rows[z].astype(jnp.int32).astype(jnp.float32) * scale
                out[...] = jnp.where(odd_ref[0] == 1, total[:, shift : shift + width], total[:, :width])

    specs, ins = [], []
    for part, m, first, count in zip(parts, PARTS, firsts, counts, strict=True):
        window = part.shape[2]

        def where(i, first=first, count=count):
            return 0, jnp.clip(i - first, 0, count - 1), 0

        def below(i, m=m):
            return 0, m // 16, 0

        specs += [pl.BlockSpec((SIDE, STEP, window), where), pl.BlockSpec((SIDE, 16, window), below)]
        ins += [part, part]
    return pl.pallas_call(
        kernel,
        grid=(sum(counts),),
        in_specs=[SMEM] + specs,
        out_specs=pl.BlockSpec((STEP, width), lambda i: (i, 0)),
        out_shape=jax.ShapeDtypeStruct((sum(PARTS), width), jnp.float32),
        compiler_params=params(60),
        name="finish",
    )(odd, *ins)


def body(hidden_rows, lengths, balance, cotangent):
    role_count = lax.axis_size("role")
    dev_count = lax.axis_size("dev")
    role, dev = lax.axis_index("role"), lax.axis_index("dev")
    z, core, y, x = role // 2, role % 2, dev // SIDE, dev % SIDE
    tok_count, width_in = hidden_rows.shape
    seq_count = lengths.shape[1]
    slot_len = tok_count // seq_count
    block_count = balance.shape[0]
    block_rows = tok_count // block_count
    pair_count = cotangent.shape[0] // role_count
    slice_width = width_in // dev_count
    shift = slice_width % 128
    starts = [slice_width * d - shift * (d % 2) for d in range(dev_count)]

    steps = [(dz, flip) for dz in range(SIDE) for flip in range(2)]
    ahead = jnp.stack([(z + dz) % SIDE * 2 + (core + flip) % 2 for dz, flip in steps])
    behind = jnp.stack([(z - dz) % SIDE * 2 + (core + flip) % 2 for dz, flip in steps])
    blocks = sort_blocks(cotangent, ahead)
    blocks = [blocks[0]] + [
        lax.ppermute(block, "role", along_z(*step))
        for block, step in zip(blocks[1:], steps[1:], strict=True)
    ]

    groups = balance[:, 0]
    onehot = (groups[:, None] == jnp.arange(role_count, dtype=jnp.int32)[None, :]).astype(jnp.int32)
    earlier = jnp.cumsum(onehot, axis=0) - onehot
    block_rank = jnp.sum(earlier * onehot, axis=1)
    token = jnp.arange(tok_count, dtype=jnp.int32)
    row_of_token = jnp.repeat(block_rank, block_rows) * block_rows + token % block_rows
    group_of_token = jnp.repeat(groups, block_rows)
    keeping = token % slot_len < jnp.repeat(lengths[0], slot_len)
    rows = jnp.arange(pair_count, dtype=jnp.int32)
    places = (
        (behind[:, None, None] == group_of_token[None, None, :])
        & (rows[None, :, None] == row_of_token[None, None, :])
        & keeping[None, None, :]
    ).astype(jnp.bfloat16)

    def exchange(cut):
        return lax.all_to_all(cut, "dev", split_axis=0, concat_axis=0, tiled=True)

    early = exchange(cut_windows(hidden_rows, starts, SPANS[0]))
    late = cut_windows(hidden_rows, [start + SPANS[0] for start in starts], SPANS[1])
    paired = pair_rows(core.reshape(1), blocks, places, early, late)
    gathered = [lax.all_gather(cot, "dev", axis=0, tiled=False) for cot in paired]
    features = [early, exchange(hold(late, paired[0]))]

    planes = [[2 * i + c for i in range(SIDE)] for c in range(2)]
    coded, came = [], []
    for cot in gathered:
        other, own = multiply(cot, features, *came[-1:])
        got = lax.ppermute(other, "role", along_z(0, 1))
        coded.append(code(own, got, *came[-2:-1]))
        came.append(
            lax.all_to_all(
                coded[-1], "role", split_axis=0, concat_axis=0, axis_index_groups=planes, tiled=True
            )
        )
    return finish(came, (dev % 2).reshape(1), shift, slice_width)


def solution(mesh):
    in_specs = (
        P(("role", "dev"), None),
        P(("role", "dev"), None),
        P(("role", "dev"), None),
        P(("role", "dev"), None),
    )
    out_specs = P("role", "dev")
    return jax.shard_map(body, mesh=mesh, in_specs=in_specs, out_specs=out_specs, check_vma=False)
```

```python
import jax
import jax.numpy as jnp
from jax import lax
from jax.experimental import pallas as pl
from jax.experimental.pallas import tpu as pltpu
from jax.sharding import PartitionSpec as P

PARTS = (224, 224)
STEP = 112
SPANS = (512, 896)
FINE = 256.0
TOP = 32767.0
SIDE = 4
VMEM = pl.BlockSpec(memory_space=pltpu.VMEM)
SMEM = pl.BlockSpec(memory_space=pltpu.SMEM)
ANY = pl.BlockSpec(memory_space=pl.ANY)
TINY = pl.CostEstimate(flops=1, bytes_accessed=1, transcendentals=0)


def params(mib):
    return pltpu.CompilerParams(vmem_limit_bytes=mib * 1024 * 1024)


def along_z(step, flip=0):
    return [
        (z * 2 + c, (z + step) % SIDE * 2 + (c + flip) % 2) for z in range(SIDE) for c in range(2)
    ]


def cut_windows(hidden_rows, starts, width):
    tok_count, width_in = hidden_rows.shape
    tile = 32

    def kernel(rows_ref, out_ref):
        for d, start in enumerate(starts):
            out_ref[d] = rows_ref[:, start : start + width]

    return pl.pallas_call(
        kernel,
        grid=(tok_count // tile,),
        in_specs=[pl.BlockSpec((tile, width_in), lambda i: (i, 0))],
        out_specs=pl.BlockSpec((len(starts), tile, width), lambda i: (0, i, 0)),
        out_shape=jax.ShapeDtypeStruct((len(starts), tok_count, width), hidden_rows.dtype),
        compiler_params=params(60),
        name="cut_windows",
    )(hidden_rows)


def hold(value, awaited):
    def kernel(value_ref, awaited_ref, out_ref):
        pass

    return pl.pallas_call(
        kernel,
        in_specs=[ANY, ANY],
        out_specs=ANY,
        out_shape=jax.ShapeDtypeStruct(value.shape, value.dtype),
        input_output_aliases={0: 0},
        compiler_params=params(60),
        cost_estimate=TINY,
        name="hold",
    )(value, awaited)


def sort_blocks(cotangent, targets):
    rows, width = cotangent.shape
    count = targets.shape[0]
    block = rows // count

    def kernel(targets_ref, cot_ref, *out_refs):
        row = lax.broadcasted_iota(jnp.int32, (block, rows), 0)
        column = lax.broadcasted_iota(jnp.int32, (block, rows), 1)
        for j in range(count):
            taking = (column == row + targets_ref[j] * block).astype(jnp.bfloat16)
            out_refs[j][...] = jnp.dot(
                taking, cot_ref[...], preferred_element_type=jnp.float32
            ).astype(jnp.bfloat16)

    return pl.pallas_call(
        kernel,
        in_specs=[SMEM, VMEM],
        out_specs=[VMEM] * count,
        out_shape=[jax.ShapeDtypeStruct((block, width), cotangent.dtype)] * count,
        compiler_params=params(60),
        name="sort_blocks",
    )(targets, cotangent)


def pair_rows(core, blocks, places, *awaited):
    block, width = blocks[0].shape
    count = len(blocks)
    tok_count = places.shape[2]
    share = width // count

    def kernel(core_ref, places_ref, *refs):
        ins, outs = refs[:count], refs[-len(PARTS) :]
        z = pl.program_id(0)
        total = jnp.zeros((2 * share, tok_count), jnp.float32)
        for j in range(count):
            total += lax.dot_general(
                ins[j][...],
                places_ref[j],
                (((0,), (0,)), ((), ())),
                preferred_element_type=jnp.float32,
            )
        total = total.astype(jnp.bfloat16)
        for q in range(2):
            own = jnp.where(core_ref[0] == q, 1, 0)
            at = q * share
            for m, out in zip(PARTS, outs, strict=True):
                to = pl.multiple_of((own * SIDE + z) * m, 16)
                out[pl.ds(to, m)] = total[at : at + m]
                at += m

    return pl.pallas_call(
        kernel,
        grid=(SIDE,),
        in_specs=[SMEM, pl.BlockSpec((count, block, tok_count), lambda i: (0, 0, 0))]
        + [pl.BlockSpec((block, 2 * share), lambda i: (0, i))] * count
        + [ANY] * len(awaited),
        out_specs=[pl.BlockSpec((count * m, tok_count), lambda i: (0, 0)) for m in PARTS],
        out_shape=[jax.ShapeDtypeStruct((count * m, tok_count), jnp.bfloat16) for m in PARTS],
        compiler_params=params(60),
        name="pair_rows",
    )(core, places, *blocks, *awaited)


def multiply(cot, features, core, *awaited):
    source_count, rows, tok_count = cot.shape
    width = sum(f.shape[2] for f in features)
    steps = 2
    tile = rows // (2 * steps)

    def kernel(cot_ref, *refs):
        out = refs[-1]
        left = jnp.concatenate([cot_ref[i] for i in range(source_count)], axis=1)
        at = 0
        for f_ref in refs[: len(features)]:
            span = f_ref.shape[2]
            right = f_ref[...].reshape(source_count * tok_count, span)
            out[:, at : at + span] = jnp.dot(left, right, preferred_element_type=jnp.float32)
            at += span

    return pl.pallas_call(
        kernel,
        grid=(steps,),
        in_specs=[pl.BlockSpec((source_count, tile, tok_count), lambda i: (0, core * steps + i, 0))]
        + [pl.BlockSpec(f.shape, lambda i: (0, 0, 0)) for f in features]
        + [ANY] * len(awaited),
        out_specs=pl.BlockSpec((tile, width), lambda i: (i, 0)),
        out_shape=jax.ShapeDtypeStruct((steps * tile, width), jnp.float32),
        compiler_params=params(24),
        cost_estimate=TINY,
        name="multiply",
    )(cot, *features, *awaited)


def code(own, got):
    rows, width = own.shape
    m = rows // SIDE

    def kernel(own_ref, got_ref, out):
        total = own_ref[...] + got_ref[...]
        largest = jnp.max(jnp.abs(total), axis=0, keepdims=True)
        level = jnp.ceil(jnp.log2(jnp.maximum(largest, 2.0**-125)) * FINE) + 1.0
        scaled = (total * jnp.exp2(level * (-1.0 / FINE))) * TOP
        coded = jnp.round(jnp.clip(scaled, -TOP, TOP)).astype(jnp.int32)
        out[0, :m] = coded.astype(jnp.int16)
        out[0, m:] = jnp.broadcast_to(level.astype(jnp.int32), (16, width)).astype(jnp.int16)

    return pl.pallas_call(
        kernel,
        grid=(SIDE,),
        in_specs=[pl.BlockSpec((m, width), lambda i: (i, 0))] * 2,
        out_specs=pl.BlockSpec((1, m + 16, width), lambda i: (i, 0, 0)),
        out_shape=jax.ShapeDtypeStruct((SIDE, m + 16, width), jnp.int16),
        compiler_params=params(24),
        cost_estimate=TINY,
        name="code",
    )(own, got)


def decode(part, p, odd, shift, width, whole):
    m = PARTS[p]
    first = sum(PARTS[:p]) // STEP
    window = part.shape[2]

    def kernel(odd_ref, rows, levels, *refs):
        total = 0.0
        for z in range(SIDE):
            level = levels[z].astype(jnp.int32).astype(jnp.float32)[:1]
            scale = jnp.exp2(level * (1.0 / FINE)) * (1.0 / TOP)
            total = total + rows[z].astype(jnp.int32).astype(jnp.float32) * scale
        refs[-1][...] = jnp.where(odd_ref[0] == 1, total[:, shift : shift + width], total[:, :width])

    held = [] if whole is None else [whole]
    return pl.pallas_call(
        kernel,
        grid=(m // STEP,),
        in_specs=[
            SMEM,
            pl.BlockSpec((SIDE, STEP, window), lambda i: (0, i, 0)),
            pl.BlockSpec((SIDE, 16, window), lambda i: (0, m // 16, 0)),
        ]
        + [ANY] * len(held),
        out_specs=pl.BlockSpec((STEP, width), lambda i: (first + i, 0)),
        out_shape=jax.ShapeDtypeStruct((sum(PARTS), width), jnp.float32),
        input_output_aliases={3: 0} if held else {},
        compiler_params=params(24),
        cost_estimate=TINY,
        name="decode",
    )(odd, part, part, *held)


def body(hidden_rows, lengths, balance, cotangent):
    role_count = lax.axis_size("role")
    dev_count = lax.axis_size("dev")
    role, dev = lax.axis_index("role"), lax.axis_index("dev")
    z, core, y, x = role // 2, role % 2, dev // SIDE, dev % SIDE
    tok_count, width_in = hidden_rows.shape
    seq_count = lengths.shape[1]
    slot_len = tok_count // seq_count
    block_count = balance.shape[0]
    block_rows = tok_count // block_count
    pair_count = cotangent.shape[0] // role_count
    slice_width = width_in // dev_count
    shift = slice_width % 128
    starts = [slice_width * d - shift * (d % 2) for d in range(dev_count)]

    steps = [(dz, flip) for dz in range(SIDE) for flip in range(2)]
    ahead = jnp.stack([(z + dz) % SIDE * 2 + (core + flip) % 2 for dz, flip in steps])
    behind = jnp.stack([(z - dz) % SIDE * 2 + (core + flip) % 2 for dz, flip in steps])
    blocks = sort_blocks(cotangent, ahead)
    blocks = [blocks[0]] + [
        lax.ppermute(block, "role", along_z(*step))
        for block, step in zip(blocks[1:], steps[1:], strict=True)
    ]

    groups = balance[:, 0]
    onehot = (groups[:, None] == jnp.arange(role_count, dtype=jnp.int32)[None, :]).astype(jnp.int32)
    earlier = jnp.cumsum(onehot, axis=0) - onehot
    block_rank = jnp.sum(earlier * onehot, axis=1)
    token = jnp.arange(tok_count, dtype=jnp.int32)
    row_of_token = jnp.repeat(block_rank, block_rows) * block_rows + token % block_rows
    group_of_token = jnp.repeat(groups, block_rows)
    keeping = token % slot_len < jnp.repeat(lengths[0], slot_len)
    rows = jnp.arange(pair_count, dtype=jnp.int32)
    places = (
        (behind[:, None, None] == group_of_token[None, None, :])
        & (rows[None, :, None] == row_of_token[None, None, :])
        & keeping[None, None, :]
    ).astype(jnp.bfloat16)

    def exchange(cut):
        return lax.all_to_all(cut, "dev", split_axis=0, concat_axis=0, tiled=True)

    early = exchange(cut_windows(hidden_rows, starts, SPANS[0]))
    late = cut_windows(hidden_rows, [start + SPANS[0] for start in starts], SPANS[1])
    paired = pair_rows(core.reshape(1), blocks, places, early, late)
    gathered = [lax.all_gather(cot, "dev", axis=0, tiled=False) for cot in paired]
    features = [early, exchange(hold(late, paired[0]))]

    planes = [[2 * i + c for i in range(SIDE)] for c in range(2)]
    whole, came = None, None
    for p, cot in enumerate(gathered):
        other = multiply(cot, features, 0, *([] if came is None else [came]))
        got = lax.ppermute(other, "role", along_z(0, 1))
        own = multiply(cot, features, 1, other)
        came = lax.all_to_all(
            code(own, got), "role", split_axis=0, concat_axis=0, axis_index_groups=planes, tiled=True
        )
        whole = decode(came, p, (dev % 2).reshape(1), shift, slice_width, whole)
    return whole


def solution(mesh):
    in_specs = (
        P(("role", "dev"), None),
        P(("role", "dev"), None),
        P(("role", "dev"), None),
        P(("role", "dev"), None),
    )
    out_specs = P("role", "dev")
    return jax.shard_map(body, mesh=mesh, in_specs=in_specs, out_specs=out_specs, check_vma=False)
```

```python
import jax
import jax.numpy as jnp
from jax import lax
from jax.experimental import pallas as pl
from jax.experimental.pallas import tpu as pltpu
from jax.sharding import PartitionSpec as P

PARTS = (256, 192)
STEP = 64
SPANS = (512, 896)
FINE = 256.0
TOP = 32767.0
SIDE = 4
PLACE = 32
VMEM = pl.BlockSpec(memory_space=pltpu.VMEM)
SMEM = pl.BlockSpec(memory_space=pltpu.SMEM)
ANY = pl.BlockSpec(memory_space=pl.ANY)
TINY = pl.CostEstimate(flops=1, bytes_accessed=1, transcendentals=0)


def params(mib):
    return pltpu.CompilerParams(vmem_limit_bytes=mib * 1024 * 1024)


def along_z(step, flip=0):
    return [
        (z * 2 + c, (z + step) % SIDE * 2 + (c + flip) % 2) for z in range(SIDE) for c in range(2)
    ]


def cut_windows(hidden_rows, starts, width):
    tok_count, width_in = hidden_rows.shape
    tile = 32

    def kernel(rows_ref, out_ref):
        for d, start in enumerate(starts):
            out_ref[d] = rows_ref[:, start : start + width]

    return pl.pallas_call(
        kernel,
        grid=(tok_count // tile,),
        in_specs=[pl.BlockSpec((tile, width_in), lambda i: (i, 0))],
        out_specs=pl.BlockSpec((len(starts), tile, width), lambda i: (0, i, 0)),
        out_shape=jax.ShapeDtypeStruct((len(starts), tok_count, width), hidden_rows.dtype),
        compiler_params=params(60),
        name="cut_windows",
    )(hidden_rows)


def hold(value, awaited):
    def kernel(value_ref, awaited_ref, out_ref):
        pass

    return pl.pallas_call(
        kernel,
        in_specs=[ANY, ANY],
        out_specs=ANY,
        out_shape=jax.ShapeDtypeStruct(value.shape, value.dtype),
        input_output_aliases={0: 0},
        compiler_params=params(60),
        cost_estimate=TINY,
        name="hold",
    )(value, awaited)


def sort_blocks(cotangent, targets):
    rows, width = cotangent.shape
    count = targets.shape[0]
    block = rows // count

    def kernel(targets_ref, cot_ref, *out_refs):
        row = lax.broadcasted_iota(jnp.int32, (block, rows), 0)
        column = lax.broadcasted_iota(jnp.int32, (block, rows), 1)
        for j in range(count):
            taking = (column == row + targets_ref[j] * block).astype(jnp.bfloat16)
            out_refs[j][...] = jnp.dot(
                taking, cot_ref[...], preferred_element_type=jnp.float32
            ).astype(jnp.bfloat16)

    return pl.pallas_call(
        kernel,
        in_specs=[SMEM, VMEM],
        out_specs=[VMEM] * count,
        out_shape=[jax.ShapeDtypeStruct((block, width), cotangent.dtype)] * count,
        compiler_params=params(60),
        name="sort_blocks",
    )(targets, cotangent)


def pair_rows(core, blocks, places, *awaited):
    block, width = blocks[0].shape
    count = len(blocks)
    tok_count = places.shape[2]
    share = width // count

    def kernel(core_ref, places_ref, *refs):
        ins, outs = refs[:count], refs[-1 - len(PARTS) : -1]
        z = pl.program_id(0)
        stacked = refs[-1]

        @pl.when(z == 0)
        def _():
            stacked[...] = jnp.zeros_like(stacked)

        for j in range(count):
            stacked[j * PLACE : j * PLACE + block] = ins[j][...]
        total = lax.dot_general(
            stacked[...],
            places_ref[...].reshape(count * PLACE, tok_count),
            (((0,), (0,)), ((), ())),
            preferred_element_type=jnp.float32,
        )
        total = total.astype(jnp.bfloat16)
        for q in range(2):
            own = jnp.where(core_ref[0] == q, 1, 0)
            at = q * share
            for m, out in zip(PARTS, outs, strict=True):
                to = pl.multiple_of((own * SIDE + z) * m, 16)
                out[pl.ds(to, m)] = total[at : at + m]
                at += m

    return pl.pallas_call(
        kernel,
        grid=(SIDE,),
        in_specs=[SMEM, pl.BlockSpec((count, PLACE, tok_count), lambda i: (0, 0, 0))]
        + [pl.BlockSpec((block, 2 * share), lambda i: (0, i))] * count
        + [ANY] * len(awaited),
        out_specs=[pl.BlockSpec((count * m, tok_count), lambda i: (0, 0)) for m in PARTS],
        out_shape=[jax.ShapeDtypeStruct((count * m, tok_count), jnp.bfloat16) for m in PARTS],
        scratch_shapes=[pltpu.VMEM((count * PLACE, 2 * share), jnp.bfloat16)],
        compiler_params=params(60),
        name="pair_rows",
    )(core, places, *blocks, *awaited)


def multiply(cot, features, core, *awaited):
    source_count, rows, tok_count = cot.shape
    width = sum(f.shape[2] for f in features)
    steps = 2
    tile = rows // (2 * steps)

    def kernel(cot_ref, *refs):
        out = refs[-1]
        left = jnp.concatenate([cot_ref[i] for i in range(source_count)], axis=1)
        at = 0
        for f_ref in refs[: len(features)]:
            span = f_ref.shape[2]
            right = f_ref[...].reshape(source_count * tok_count, span)
            out[:, at : at + span] = jnp.dot(left, right, preferred_element_type=jnp.float32)
            at += span

    return pl.pallas_call(
        kernel,
        grid=(steps,),
        in_specs=[pl.BlockSpec((source_count, tile, tok_count), lambda i: (0, core * steps + i, 0))]
        + [pl.BlockSpec(f.shape, lambda i: (0, 0, 0)) for f in features]
        + [ANY] * len(awaited),
        out_specs=pl.BlockSpec((tile, width), lambda i: (i, 0)),
        out_shape=jax.ShapeDtypeStruct((steps * tile, width), jnp.float32),
        compiler_params=params(24),
        cost_estimate=TINY,
        name="multiply",
    )(cot, *features, *awaited)


def code(own, got):
    rows, width = own.shape
    m = rows // SIDE

    def kernel(own_ref, got_ref, out):
        total = own_ref[...] + got_ref[...]
        largest = jnp.max(jnp.abs(total), axis=0, keepdims=True)
        level = jnp.ceil(jnp.log2(jnp.maximum(largest, 2.0**-125)) * FINE) + 1.0
        scaled = (total * jnp.exp2(level * (-1.0 / FINE))) * TOP
        coded = jnp.round(jnp.clip(scaled, -TOP, TOP)).astype(jnp.int32)
        out[0, :m] = coded.astype(jnp.int16)
        out[0, m:] = jnp.broadcast_to(level.astype(jnp.int32), (16, width)).astype(jnp.int16)

    return pl.pallas_call(
        kernel,
        grid=(SIDE,),
        in_specs=[pl.BlockSpec((m, width), lambda i: (i, 0))] * 2,
        out_specs=pl.BlockSpec((1, m + 16, width), lambda i: (i, 0, 0)),
        out_shape=jax.ShapeDtypeStruct((SIDE, m + 16, width), jnp.int16),
        compiler_params=params(24),
        cost_estimate=TINY,
        name="code",
    )(own, got)


def decode(part, p, odd, shift, width, whole):
    m = PARTS[p]
    first = sum(PARTS[:p]) // STEP
    window = part.shape[2]

    def kernel(odd_ref, rows, levels, *refs):
        total = 0.0
        for z in range(SIDE):
            level = levels[z].astype(jnp.int32).astype(jnp.float32)[:1]
            scale = jnp.exp2(level * (1.0 / FINE)) * (1.0 / TOP)
            total = total + rows[z].astype(jnp.int32).astype(jnp.float32) * scale
        refs[-1][...] = jnp.where(odd_ref[0] == 1, total[:, shift : shift + width], total[:, :width])

    held = [] if whole is None else [whole]
    return pl.pallas_call(
        kernel,
        grid=(m // STEP,),
        in_specs=[
            SMEM,
            pl.BlockSpec((SIDE, STEP, window), lambda i: (0, i, 0)),
            pl.BlockSpec((SIDE, 16, window), lambda i: (0, m // 16, 0)),
        ]
        + [ANY] * len(held),
        out_specs=pl.BlockSpec((STEP, width), lambda i: (first + i, 0)),
        out_shape=jax.ShapeDtypeStruct((sum(PARTS), width), jnp.float32),
        input_output_aliases={3: 0} if held else {},
        compiler_params=params(24),
        cost_estimate=TINY,
        name="decode",
    )(odd, part, part, *held)


def body(hidden_rows, lengths, balance, cotangent):
    role_count = lax.axis_size("role")
    dev_count = lax.axis_size("dev")
    role, dev = lax.axis_index("role"), lax.axis_index("dev")
    z, core, y, x = role // 2, role % 2, dev // SIDE, dev % SIDE
    tok_count, width_in = hidden_rows.shape
    seq_count = lengths.shape[1]
    slot_len = tok_count // seq_count
    block_count = balance.shape[0]
    block_rows = tok_count // block_count
    pair_count = cotangent.shape[0] // role_count
    slice_width = width_in // dev_count
    shift = slice_width % 128
    starts = [slice_width * d - shift * (d % 2) for d in range(dev_count)]

    steps = [(dz, flip) for dz in range(SIDE) for flip in range(2)]
    ahead = jnp.stack([(z + dz) % SIDE * 2 + (core + flip) % 2 for dz, flip in steps])
    behind = jnp.stack([(z - dz) % SIDE * 2 + (core + flip) % 2 for dz, flip in steps])
    blocks = sort_blocks(cotangent, ahead)
    blocks = [blocks[0]] + [
        lax.ppermute(block, "role", along_z(*step))
        for block, step in zip(blocks[1:], steps[1:], strict=True)
    ]

    groups = balance[:, 0]
    onehot = (groups[:, None] == jnp.arange(role_count, dtype=jnp.int32)[None, :]).astype(jnp.int32)
    earlier = jnp.cumsum(onehot, axis=0) - onehot
    block_rank = jnp.sum(earlier * onehot, axis=1)
    token = jnp.arange(tok_count, dtype=jnp.int32)
    row_of_token = jnp.repeat(block_rank, block_rows) * block_rows + token % block_rows
    group_of_token = jnp.repeat(groups, block_rows)
    keeping = token % slot_len < jnp.repeat(lengths[0], slot_len)
    rows = jnp.arange(PLACE, dtype=jnp.int32)
    places = (
        (behind[:, None, None] == group_of_token[None, None, :])
        & (rows[None, :, None] == row_of_token[None, None, :])
        & keeping[None, None, :]
    ).astype(jnp.bfloat16)

    def exchange(cut):
        return lax.all_to_all(cut, "dev", split_axis=0, concat_axis=0, tiled=True)

    early = exchange(cut_windows(hidden_rows, starts, SPANS[0]))
    late = cut_windows(hidden_rows, [start + SPANS[0] for start in starts], SPANS[1])
    paired = pair_rows(core.reshape(1), blocks, places, early, late)
    gathered = [lax.all_gather(cot, "dev", axis=0, tiled=False) for cot in paired]
    features = [early, exchange(hold(late, paired[0]))]

    planes = [[2 * i + c for i in range(SIDE)] for c in range(2)]
    whole, came = None, None
    for p, cot in enumerate(gathered):
        other = multiply(cot, features, 0, *([] if came is None else [came]))
        got = lax.ppermute(other, "role", along_z(0, 1))
        own = multiply(cot, features, 1, other)
        came = lax.all_to_all(
            code(own, got), "role", split_axis=0, concat_axis=0, axis_index_groups=planes, tiled=True
        )
        whole = decode(came, p, (dev % 2).reshape(1), shift, slice_width, whole)
    return whole


def solution(mesh):
    in_specs = (
        P(("role", "dev"), None),
        P(("role", "dev"), None),
        P(("role", "dev"), None),
        P(("role", "dev"), None),
    )
    out_specs = P("role", "dev")
    return jax.shard_map(body, mesh=mesh, in_specs=in_specs, out_specs=out_specs, check_vma=False)
```

```python
import jax
import jax.numpy as jnp
from jax import lax
from jax.experimental import pallas as pl
from jax.experimental.pallas import tpu as pltpu
from jax.sharding import PartitionSpec as P

PARTS = (256, 192)
STEP = 64
SPANS = (512, 896)
FINE = 256.0
TOP = 32767.0
SIDE = 4
PLACE = 32
VMEM = pl.BlockSpec(memory_space=pltpu.VMEM)
SMEM = pl.BlockSpec(memory_space=pltpu.SMEM)
ANY = pl.BlockSpec(memory_space=pl.ANY)
TINY = pl.CostEstimate(flops=1, bytes_accessed=1, transcendentals=0)


def params(mib):
    return pltpu.CompilerParams(vmem_limit_bytes=mib * 1024 * 1024)


def along_z(step, flip=0):
    return [
        (z * 2 + c, (z + step) % SIDE * 2 + (c + flip) % 2) for z in range(SIDE) for c in range(2)
    ]


def cut_windows(hidden_rows, starts, width):
    tok_count, width_in = hidden_rows.shape
    tile = 32

    def kernel(rows_ref, out_ref):
        for d, start in enumerate(starts):
            out_ref[d] = rows_ref[:, start : start + width]

    return pl.pallas_call(
        kernel,
        grid=(tok_count // tile,),
        in_specs=[pl.BlockSpec((tile, width_in), lambda i: (i, 0))],
        out_specs=pl.BlockSpec((len(starts), tile, width), lambda i: (0, i, 0)),
        out_shape=jax.ShapeDtypeStruct((len(starts), tok_count, width), hidden_rows.dtype),
        compiler_params=params(60),
        name="cut_windows",
    )(hidden_rows)


def hold(value, awaited):
    def kernel(value_ref, awaited_ref, out_ref):
        pass

    return pl.pallas_call(
        kernel,
        in_specs=[ANY, ANY],
        out_specs=ANY,
        out_shape=jax.ShapeDtypeStruct(value.shape, value.dtype),
        input_output_aliases={0: 0},
        compiler_params=params(60),
        cost_estimate=TINY,
        name="hold",
    )(value, awaited)


def sort_blocks(cotangent, targets):
    rows, width = cotangent.shape
    count = targets.shape[0]
    block = rows // count

    def kernel(targets_ref, cot_ref, *out_refs):
        row = lax.broadcasted_iota(jnp.int32, (PLACE, rows), 0)
        column = lax.broadcasted_iota(jnp.int32, (PLACE, rows), 1)
        taking = jnp.concatenate(
            [(column == row + targets_ref[j] * block).astype(jnp.bfloat16) for j in range(count)]
        )
        taken = jnp.dot(taking, cot_ref[...], preferred_element_type=jnp.float32)
        for j, out_ref in enumerate(out_refs):
            out_ref[...] = taken[j * PLACE : j * PLACE + block].astype(jnp.bfloat16)

    return pl.pallas_call(
        kernel,
        in_specs=[SMEM, VMEM],
        out_specs=[VMEM] * count,
        out_shape=[jax.ShapeDtypeStruct((block, width), cotangent.dtype)] * count,
        compiler_params=params(60),
        name="sort_blocks",
    )(targets, cotangent)


def pair_rows(core, blocks, places, *awaited):
    block, width = blocks[0].shape
    count = len(blocks)
    tok_count = places.shape[2]
    share = width // count

    def kernel(core_ref, places_ref, *refs):
        ins, outs = refs[:count], refs[-1 - len(PARTS) : -1]
        z = pl.program_id(0)
        stacked = refs[-1]

        @pl.when(z == 0)
        def _():
            stacked[...] = jnp.zeros_like(stacked)

        for j in range(count):
            stacked[j * PLACE : j * PLACE + block] = ins[j][...]
        total = lax.dot_general(
            stacked[...],
            places_ref[...].reshape(count * PLACE, tok_count),
            (((0,), (0,)), ((), ())),
            preferred_element_type=jnp.float32,
        )
        total = total.astype(jnp.bfloat16)
        for q in range(2):
            own = jnp.where(core_ref[0] == q, 1, 0)
            at = q * share
            for m, out in zip(PARTS, outs, strict=True):
                to = pl.multiple_of((own * SIDE + z) * m, 16)
                out[pl.ds(to, m)] = total[at : at + m]
                at += m

    return pl.pallas_call(
        kernel,
        grid=(SIDE,),
        in_specs=[SMEM, pl.BlockSpec((count, PLACE, tok_count), lambda i: (0, 0, 0))]
        + [pl.BlockSpec((block, 2 * share), lambda i: (0, i))] * count
        + [ANY] * len(awaited),
        out_specs=[pl.BlockSpec((count * m, tok_count), lambda i: (0, 0)) for m in PARTS],
        out_shape=[jax.ShapeDtypeStruct((count * m, tok_count), jnp.bfloat16) for m in PARTS],
        scratch_shapes=[pltpu.VMEM((count * PLACE, 2 * share), jnp.bfloat16)],
        compiler_params=params(60),
        name="pair_rows",
    )(core, places, *blocks, *awaited)


def multiply(cot, features, core, *awaited):
    source_count, rows, tok_count = cot.shape
    width = sum(f.shape[2] for f in features)
    steps = 1
    tile = rows // (2 * steps)

    def kernel(cot_ref, *refs):
        out = refs[-1]
        left = jnp.concatenate([cot_ref[i] for i in range(source_count)], axis=1)
        at = 0
        for f_ref in refs[: len(features)]:
            span = f_ref.shape[2]
            right = f_ref[...].reshape(source_count * tok_count, span)
            out[:, at : at + span] = jnp.dot(left, right, preferred_element_type=jnp.float32)
            at += span

    return pl.pallas_call(
        kernel,
        grid=(steps,),
        in_specs=[pl.BlockSpec((source_count, tile, tok_count), lambda i: (0, core * steps + i, 0))]
        + [pl.BlockSpec(f.shape, lambda i: (0, 0, 0)) for f in features]
        + [ANY] * len(awaited),
        out_specs=pl.BlockSpec((tile, width), lambda i: (i, 0)),
        out_shape=jax.ShapeDtypeStruct((steps * tile, width), jnp.float32),
        compiler_params=params(24),
        cost_estimate=TINY,
        name="multiply",
    )(cot, *features, *awaited)


def code(own, got):
    rows, width = own.shape
    m = rows // SIDE

    def kernel(own_ref, got_ref, out):
        total = own_ref[...] + got_ref[...]
        largest = jnp.max(jnp.abs(total), axis=0, keepdims=True)
        level = jnp.ceil(jnp.log2(jnp.maximum(largest, 2.0**-125)) * FINE) + 1.0
        scaled = (total * jnp.exp2(level * (-1.0 / FINE))) * TOP
        coded = jnp.round(jnp.clip(scaled, -TOP, TOP)).astype(jnp.int32)
        out[0, :m] = coded.astype(jnp.int16)
        out[0, m:] = jnp.broadcast_to(level.astype(jnp.int32), (16, width)).astype(jnp.int16)

    return pl.pallas_call(
        kernel,
        grid=(SIDE,),
        in_specs=[pl.BlockSpec((m, width), lambda i: (i, 0))] * 2,
        out_specs=pl.BlockSpec((1, m + 16, width), lambda i: (i, 0, 0)),
        out_shape=jax.ShapeDtypeStruct((SIDE, m + 16, width), jnp.int16),
        compiler_params=params(24),
        cost_estimate=TINY,
        name="code",
    )(own, got)


def decode(part, p, odd, shift, width, whole):
    m = PARTS[p]
    first = sum(PARTS[:p]) // STEP
    window = part.shape[2]

    def kernel(odd_ref, rows, levels, *refs):
        total = 0.0
        for z in range(SIDE):
            level = levels[z].astype(jnp.int32).astype(jnp.float32)[:1]
            scale = jnp.exp2(level * (1.0 / FINE)) * (1.0 / TOP)
            total = total + rows[z].astype(jnp.int32).astype(jnp.float32) * scale
        refs[-1][...] = jnp.where(odd_ref[0] == 1, total[:, shift : shift + width], total[:, :width])

    held = [] if whole is None else [whole]
    return pl.pallas_call(
        kernel,
        grid=(m // STEP,),
        in_specs=[
            SMEM,
            pl.BlockSpec((SIDE, STEP, window), lambda i: (0, i, 0)),
            pl.BlockSpec((SIDE, 16, window), lambda i: (0, m // 16, 0)),
        ]
        + [ANY] * len(held),
        out_specs=pl.BlockSpec((STEP, width), lambda i: (first + i, 0)),
        out_shape=jax.ShapeDtypeStruct((sum(PARTS), width), jnp.float32),
        input_output_aliases={3: 0} if held else {},
        compiler_params=params(24),
        cost_estimate=TINY,
        name="decode",
    )(odd, part, part, *held)


def body(hidden_rows, lengths, balance, cotangent):
    role_count = lax.axis_size("role")
    dev_count = lax.axis_size("dev")
    role, dev = lax.axis_index("role"), lax.axis_index("dev")
    z, core, y, x = role // 2, role % 2, dev // SIDE, dev % SIDE
    tok_count, width_in = hidden_rows.shape
    seq_count = lengths.shape[1]
    slot_len = tok_count // seq_count
    block_count = balance.shape[0]
    block_rows = tok_count // block_count
    pair_count = cotangent.shape[0] // role_count
    slice_width = width_in // dev_count
    shift = slice_width % 128
    starts = [slice_width * d - shift * (d % 2) for d in range(dev_count)]

    steps = [(dz, flip) for dz in range(SIDE) for flip in range(2)]
    ahead = jnp.stack([(z + dz) % SIDE * 2 + (core + flip) % 2 for dz, flip in steps])
    behind = jnp.stack([(z - dz) % SIDE * 2 + (core + flip) % 2 for dz, flip in steps])
    blocks = sort_blocks(cotangent, ahead)
    blocks = [blocks[0]] + [
        lax.ppermute(block, "role", along_z(*step))
        for block, step in zip(blocks[1:], steps[1:], strict=True)
    ]

    groups = balance[:, 0]
    onehot = (groups[:, None] == jnp.arange(role_count, dtype=jnp.int32)[None, :]).astype(jnp.int32)
    earlier = jnp.cumsum(onehot, axis=0) - onehot
    block_rank = jnp.sum(earlier * onehot, axis=1)
    token = jnp.arange(tok_count, dtype=jnp.int32)
    row_of_token = jnp.repeat(block_rank, block_rows) * block_rows + token % block_rows
    group_of_token = jnp.repeat(groups, block_rows)
    keeping = token % slot_len < jnp.repeat(lengths[0], slot_len)
    rows = jnp.arange(PLACE, dtype=jnp.int32)
    places = (
        (behind[:, None, None] == group_of_token[None, None, :])
        & (rows[None, :, None] == row_of_token[None, None, :])
        & keeping[None, None, :]
    ).astype(jnp.bfloat16)

    def exchange(cut):
        return lax.all_to_all(cut, "dev", split_axis=0, concat_axis=0, tiled=True)

    early = exchange(cut_windows(hidden_rows, starts, SPANS[0]))
    late = cut_windows(hidden_rows, [start + SPANS[0] for start in starts], SPANS[1])
    paired = pair_rows(core.reshape(1), blocks, places, early, late)
    gathered = [lax.all_gather(cot, "dev", axis=0, tiled=False) for cot in paired]
    features = [early, exchange(hold(late, paired[0]))]

    planes = [[2 * i + c for i in range(SIDE)] for c in range(2)]
    whole, came = None, None
    for p, cot in enumerate(gathered):
        other = multiply(cot, features, 0, *([] if came is None else [came]))
        got = lax.ppermute(other, "role", along_z(0, 1))
        own = multiply(cot, features, 1, other)
        came = lax.all_to_all(
            code(own, got), "role", split_axis=0, concat_axis=0, axis_index_groups=planes, tiled=True
        )
        whole = decode(came, p, (dev % 2).reshape(1), shift, slice_width, whole)
    return whole


def solution(mesh):
    in_specs = (
        P(("role", "dev"), None),
        P(("role", "dev"), None),
        P(("role", "dev"), None),
        P(("role", "dev"), None),
    )
    out_specs = P("role", "dev")
    return jax.shard_map(body, mesh=mesh, in_specs=in_specs, out_specs=out_specs, check_vma=False)
```
